32 devices in a mesh: section: 2 (over core), dp: 16 (over z, y, x).
Axes of the slice: x: 2, y: 2, z: 4, core: 2. Of those that a mesh axis runs over, the one named last changes fastest.
Arguments:
- frames: float32 [2, 16, 256, 1024], P(None, 'dp')
- cotangent: float32 [2, 16, 256, 1024], P(None, 'dp'), may hold values from -6 to 6
- lengths: int32 [2, 16], P(None, 'dp'), may hold values from 1 to 256, 2560 in all within a row
- attn_in: float32 [2, 1024, 3072], P('section', 'dp')
- attn_out: float32 [2, 1024, 1024], P('section', 'dp')
- ffn_up: float32 [2, 1024, 4096], P('section', 'dp')
- ffn_down: float32 [2, 4096, 1024], P('section', 'dp')
- norm_params: float32 [2, 4, 1024], P('section', None, 'dp')
- skip_proj: float32 [2048, 1024], P(('section', 'dp'))
- in_rows: float32 [2, 1024], P('section', 'dp'), may hold values from 491.52 to 1966.08
- in_cols: float32 [2, 3072], P('section'), may hold values from 491.52 to 1966.08
- out_rows: float32 [2, 1024], P('section', 'dp'), may hold values from 98.304 to 393.216
- out_cols: float32 [2, 1024], P('section'), may hold values from 98.304 to 393.216
- up_rows: float32 [2, 1024], P('section', 'dp'), may hold values from 98.304 to 393.216
- up_cols: float32 [2, 4096], P('section'), may hold values from 98.304 to 393.216
- down_rows: float32 [2, 4096], P('section', 'dp'), may hold values from 393.216 to 1572.864
- down_cols: float32 [2, 1024], P('section'), may hold values from 393.216 to 1572.864
- skip_rows: float32 [2048], P(('section', 'dp')), may hold values from 1966.08 to 7864.32
- skip_cols: float32 [1024], replicated, may hold values from 1966.08 to 7864.32
- norm_moment: float32 [2, 4, 1024], P('section', None, 'dp'), may hold values from 983.04 to 3932.16
Outputs:
- layer_outputs: float32 [2, 2, 16, 256, 1024], P('section', None, 'dp')
- input_grads: float32 [2, 2, 16, 256, 1024], P('section', None, 'dp')
- grad_in: float32 [2, 1024, 3072], P('section', 'dp')
- rows_in: float32 [2, 1024], P('section', 'dp')
- cols_in: float32 [2, 3072], P('section')
- new_in: float32 [2, 1024, 3072], P('section', 'dp')
- grad_out: float32 [2, 1024, 1024], P('section', 'dp')
- rows_out: float32 [2, 1024], P('section', 'dp')
- cols_out: float32 [2, 1024], P('section')
- new_out: float32 [2, 1024, 1024], P('section', 'dp')
- grad_up: float32 [2, 1024, 4096], P('section', 'dp')
- rows_up: float32 [2, 1024], P('section', 'dp')
- cols_up: float32 [2, 4096], P('section')
- new_up: float32 [2, 1024, 4096], P('section', 'dp')
- grad_down: float32 [2, 4096, 1024], P('section', 'dp')
- rows_down: float32 [2, 4096], P('section', 'dp')
- cols_down: float32 [2, 1024], P('section')
- new_down: float32 [2, 4096, 1024], P('section', 'dp')
- grad_skip: float32 [2048, 1024], P(('section', 'dp'))
- rows_skip: float32 [2048], P(('section', 'dp'))
- cols_skip: float32 [1024], replicated
- new_skip: float32 [2048, 1024], P(('section', 'dp'))
- grad_norms: float32 [2, 4, 1024], P('section', None, 'dp')
- moment_norms: float32 [2, 4, 1024], P('section', None, 'dp')
- new_norms: float32 [2, 4, 1024], P('section', None, 'dp')
The draws below stay inside these ranges and needn't reach their ends.
Inputs may be any that keep to these rules, and one draw needn't show every extreme that they name: In every micro-batch the lengths sum to 2560 and one equals 256.
All inputs are finite; a program needn't handle non-finite values. No bound on the sum of `lengths` on one device may be relied on, other than what follows from the above.
Results may differ from the reference program's by a relative error of at most 0.0003.
Values sent between devices are 32-bit elements; how exact they have to be, the bound alone decides.
No kernel may reach another device: no remote copies, remote signals or barrier semaphores. Data moves between devices by JAX's collectives and lax.ppermute only.
A program may use at most 896 MiB of HBM per device.

```python
import math
import jax
import jax.numpy as jnp
import numpy as np
from jax import lax

D = 1024
FF = 4096
HEADS = 16
SEQ = 256
MICRO = 2
STEP = 10
BATCH = 16


def ramp(count, low, high):
    return low + (high - low) * jnp.arange(count, dtype=jnp.float32) / (count - 1)


def draw_frames(key, part):
    key = jax.random.fold_in(key, 11)
    shape = (MICRO, BATCH, SEQ, D)
    noise = jnp.clip(jax.random.normal(key, shape, jnp.float32), -6.0, 6.0)
    return noise * ramp(D, 0.6, 1.8)


def scaled_matrix(key, shape, scale, low, high, spread):
    return spread * ramp(shape[-1], low, high) * scale


def draw_attn_in(key, part):
    key = jax.random.fold_in(key, 12)
    shape = (2, D, 3 * D)
    noise = jnp.clip(jax.random.normal(key, shape, jnp.float32), -6.0, 6.0)
    return scaled_matrix(key, shape, D ** (-0.5), 0.6, 1.8, noise)


def draw_attn_out(key, part):
    key = jax.random.fold_in(key, 13)
    shape = (2, D, D)
    noise = jnp.clip(jax.random.normal(key, shape, jnp.float32), -6.0, 6.0)
    return scaled_matrix(key, shape, 4.0 * D ** (-0.5), 0.6, 1.8, noise)


def draw_ffn_up(key, part):
    key = jax.random.fold_in(key, 14)
    shape = (2, D, FF)
    noise = jnp.clip(jax.random.normal(key, shape, jnp.float32), -6.0, 6.0)
    return scaled_matrix(key, shape, D ** (-0.5), 0.6, 1.8, noise)


def draw_ffn_down(key, part):
    key = jax.random.fold_in(key, 15)
    shape = (2, FF, D)
    noise = jnp.clip(jax.random.normal(key, shape, jnp.float32), -6.0, 6.0)
    return scaled_matrix(key, shape, FF ** (-0.5), 0.6, 1.8, noise)


def draw_skip_proj(key, part):
    key = jax.random.fold_in(key, 16)
    shape = (2 * D, D)
    noise = jnp.clip(jax.random.normal(key, shape, jnp.float32), -6.0, 6.0)
    return scaled_matrix(key, shape, (2 * D) ** (-0.5), 0.6, 1.8, noise)


def draw_norm_params(key, part):
    key = jax.random.fold_in(key, 17)
    shape = (2, 4, D)
    gain_rows = (jnp.arange(4) % 2 == 0).astype(jnp.float32)[None, :, None]
    noise = jnp.clip(jax.random.normal(key, shape, jnp.float32), -4.0, 4.0)
    gains = ramp(D, 0.6, 1.8) * (1.0 + 0.1 * noise)
    return gain_rows * gains + (1.0 - gain_rows) * 0.2 * noise


def block_levels(key, shape, shards, low, top_value):
    def one(dim, blocks):
        heights = jax.random.uniform(jax.random.fold_in(jax.random.fold_in(key, 6), dim), (blocks,), jnp.float32, low / len(shards), top_value / len(shards))
        return jnp.repeat(jnp.exp(heights), shape[dim] // blocks).reshape((-1,) + (1,) * (len(shape) - dim - 1))

    gain = one(*shards[0])
    for cut in shards[1:]:
        gain = gain * one(*cut)
    return gain


def length_profile(amount, total, limit, lean):
    weights = [(1 << 20) // math.isqrt(standing ** lean) + 1 for standing in range(2, amount + 1)]
    spare, holding = total - limit - (amount - 1), [1] * (amount - 1)
    while spare > 0:
        movable = [i for i in range(amount - 1) if holding[i] < limit]
        mass, budget = sum([weights[i] for i in movable]), spare
        for i in movable:
            more = min(limit - holding[i], max(1, budget * weights[i] // mass), spare)
            holding[i] = holding[i] + more
            spare = spare - more
    return np.array([limit] + holding)


def ragged(key, number_of, total, bound, lean):
    if number_of == 2:
        one = jax.random.randint(key, (), max(1, total - bound), min(bound, total - 1) + 1)
        return jnp.stack([one, total - one])
    sizes = jnp.asarray(length_profile(number_of, total, bound, lean), jnp.int32)
    couples = (number_of - 1) // 2
    donor, taker = sizes[1:1 + 2 * couples:2], sizes[2:2 + 2 * couples:2]
    room = jnp.minimum(donor - 1, bound - taker)
    passed = jax.random.randint(jax.random.fold_in(key, 1), (couples,), 0, 1 << 20) % (room + 1)
    sizes = sizes.at[1:1 + 2 * couples:2].set(donor - passed).at[2:2 + 2 * couples:2].set(taker + passed)
    return sizes[jax.random.permutation(jax.random.fold_in(key, 2), number_of)]


def normal_values(stream_key, extent, scale, bound, cuts=(), kind=jnp.bfloat16):
    values = scale * jax.random.normal(stream_key, extent, jnp.float32)
    if cuts:
        values = values * block_levels(stream_key, extent, cuts, -0.22, 0.18)
    return jnp.clip(values, -bound, bound).astype(kind)


def setup_inputs(seed: int = 0) -> dict:
    key_list = jax.random.split(jax.random.key(seed), 21)
    return {
        "frames": draw_frames(jax.random.fold_in(key_list[20], 71), 0),
        "cotangent": normal_values(key_list[1], (MICRO, BATCH, SEQ, D), 1.0, 6.0, ((1, 16),), jnp.float32),
        "lengths": jax.vmap(lambda own: ragged(own, BATCH, BATCH * SEQ * 5 // 8, SEQ, 2))(jax.random.split(key_list[2], MICRO)).reshape((MICRO, BATCH)).astype(jnp.int32),
        "attn_in": draw_attn_in(jax.random.fold_in(key_list[20], 71), 0),
        "attn_out": draw_attn_out(jax.random.fold_in(key_list[20], 71), 0),
        "ffn_up": draw_ffn_up(jax.random.fold_in(key_list[20], 71), 0),
        "ffn_down": draw_ffn_down(jax.random.fold_in(key_list[20], 71), 0),
        "norm_params": draw_norm_params(jax.random.fold_in(key_list[20], 71), 0),
        "skip_proj": draw_skip_proj(jax.random.fold_in(key_list[20], 71), 0),
        "in_rows": jnp.clip(jnp.exp(math.log(1966.08) - 1.3862944 * jax.random.uniform(key_list[9], (2, D), jnp.float32) ** block_levels(key_list[9], (2, D), ((0, 2), (1, 16)), -0.2, 0.2)), 491.52, 1966.08),
        "in_cols": jnp.clip(jnp.exp(math.log(1966.08) - 1.3862944 * jax.random.uniform(key_list[10], (2, 3 * D), jnp.float32) ** block_levels(key_list[10], (2, 3 * D), ((0, 2),), -0.2, 0.2)), 491.52, 1966.08),
        "out_rows": jnp.clip(jnp.exp(math.log(393.216) - 1.3862944 * jax.random.uniform(key_list[11], (2, D), jnp.float32) ** block_levels(key_list[11], (2, D), ((0, 2), (1, 16)), -0.2, 0.2)), 98.304, 393.216),
        "out_cols": jnp.clip(jnp.exp(math.log(393.216) - 1.3862944 * jax.random.uniform(key_list[12], (2, D), jnp.float32) ** block_levels(key_list[12], (2, D), ((0, 2),), -0.2, 0.2)), 98.304, 393.216),
        "up_rows": jnp.clip(jnp.exp(math.log(393.216) - 1.3862944 * jax.random.uniform(key_list[13], (2, D), jnp.float32) ** block_levels(key_list[13], (2, D), ((0, 2), (1, 16)), -0.2, 0.2)), 98.304, 393.216),
        "up_cols": jnp.clip(jnp.exp(math.log(393.216) - 1.3862944 * jax.random.uniform(key_list[14], (2, FF), jnp.float32) ** block_levels(key_list[14], (2, FF), ((0, 2),), -0.2, 0.2)), 98.304, 393.216),
        "down_rows": jnp.clip(jnp.exp(math.log(1572.864) - 1.3862944 * jax.random.uniform(key_list[15], (2, FF), jnp.float32) ** block_levels(key_list[15], (2, FF), ((0, 2), (1, 16)), -0.2, 0.2)), 393.216, 1572.864),
        "down_cols": jnp.clip(jnp.exp(math.log(1572.864) - 1.3862944 * jax.random.uniform(key_list[16], (2, D), jnp.float32) ** block_levels(key_list[16], (2, D), ((0, 2),), -0.2, 0.2)), 393.216, 1572.864),
        "skip_rows": jnp.clip(jnp.exp(math.log(7864.32) - 1.3862944 * jax.random.uniform(key_list[17], (2 * D,), jnp.float32) ** block_levels(key_list[17], (2 * D,), ((0, 32),), -0.2, 0.2)), 1966.08, 7864.32),
        "skip_cols": jnp.clip(jnp.exp(jax.random.uniform(key_list[18], (D,), jnp.float32, math.log(1966.08), math.log(7864.32))), 1966.08, 7864.32),
        "norm_moment": jnp.clip(jnp.exp(math.log(3932.16) - 1.3862944 * jax.random.uniform(key_list[19], (2, 4, D), jnp.float32) ** block_levels(key_list[19], (2, 4, D), ((0, 2), (2, 16)), -0.2, 0.2)), 983.04, 3932.16),
    }


EPS = 1e-05
TINY = 1e-30
CLIP = 1.0
RHO = 0.5
FLOOR = 0.001
MASKED = -1e+30
HIGH = lax.Precision.HIGHEST

def layer_norm(stream, norm_gain, norm_shift):
    average = lax.optimization_barrier(jnp.mean(stream, axis=-1, keepdims=True))
    centered = stream - average
    spread = lax.optimization_barrier(jnp.mean(centered * centered, axis=-1, keepdims=True))
    return centered * lax.rsqrt(spread + EPS) * norm_gain + norm_shift

def attention(stream, norm_gain, norm_shift, w_in, w_out, length):
    frame_count, model_width = stream.shape
    head_width = model_width // HEADS
    normed = layer_norm(stream, norm_gain, norm_shift)
    projected = jnp.dot(normed, w_in, precision=HIGH).reshape(frame_count, 3, HEADS, head_width)
    query_heads = projected[:, 0]
    key_heads = projected[:, 1]
    value_heads = projected[:, 2]
    scores = jnp.einsum('qhd,khd->hqk', query_heads, key_heads, precision=HIGH) * head_width ** (-0.5)
    positions = jnp.arange(frame_count)
    distance = jnp.abs(positions[:, None] - positions[None, :]).astype(jnp.float32)
    slopes = 2.0 ** (-8.0 * (jnp.arange(HEADS).astype(jnp.float32) + 1.0) / HEADS)
    scores = scores - slopes[:, None, None] * distance[None]
    scores = jnp.where((positions < length)[None, None, :], scores, MASKED)
    row_max = lax.optimization_barrier(jnp.max(scores, axis=-1, keepdims=True))
    weighted = jnp.exp(scores - row_max)
    probability = weighted / lax.optimization_barrier(jnp.sum(weighted, axis=-1, keepdims=True))
    context = jnp.einsum('hqk,khd->qhd', probability, value_heads, precision=HIGH).reshape(frame_count, model_width)
    return stream + jnp.dot(context, w_out, precision=HIGH)

def feed_forward(stream, norm_gain, norm_shift, w_up, w_down):
    normed = layer_norm(stream, norm_gain, norm_shift)
    hidden = jax.nn.gelu(jnp.dot(normed, w_up, precision=HIGH), approximate=False)
    return stream + jnp.dot(hidden, w_down, precision=HIGH)

def utterance(params, source, probe_add, length):
    w_in, w_out, w_up, w_down, norm_set, w_skip = params
    after_attn = attention(source, norm_set[0, 0], norm_set[0, 1], w_in[0], w_out[0], length) + probe_add
    layer_twelve = feed_forward(after_attn, norm_set[1, 2], norm_set[1, 3], w_up[1], w_down[1])
    joined = jnp.dot(jnp.concatenate([layer_twelve, source], axis=-1), w_skip, precision=HIGH)
    middle = attention(joined, norm_set[1, 0], norm_set[1, 1], w_in[1], w_out[1], length)
    layer_thirteen = feed_forward(middle, norm_set[0, 2], norm_set[0, 3], w_up[0], w_down[0])
    return (layer_thirteen, layer_twelve)

def factored(grad, weight, rows, cols):
    decay = 1.0 - STEP ** (-0.8)
    squared = grad * grad + TINY
    rows_new = decay * rows + (1.0 - decay) * lax.optimization_barrier(jnp.mean(squared, axis=1))
    cols_new = decay * cols + (1.0 - decay) * lax.optimization_barrier(jnp.mean(squared, axis=0))
    second = rows_new[:, None] * cols_new[None, :] / jnp.mean(rows_new)
    update = grad * lax.rsqrt(second)
    ratio = jnp.sqrt(jnp.mean(update * update)) / CLIP
    update = update / jnp.maximum(ratio, 1.0)
    scale = jnp.maximum(jnp.sqrt(jnp.mean(weight * weight)), FLOOR)
    return (rows_new, cols_new, weight - RHO * scale * update)

def stacked_update(grad, weight, rows, cols):
    pieces = [factored(grad[member], weight[member], rows[member], cols[member]) for member in range(2)]
    return (grad, jnp.stack([pieces[0][0], pieces[1][0]]), jnp.stack([pieces[0][1], pieces[1][1]]), jnp.stack([pieces[0][2], pieces[1][2]]))

def unfactored(grad, param, moment):
    decay = 1.0 - STEP ** (-0.8)
    moment_new = decay * moment + (1.0 - decay) * (grad * grad + TINY)
    update = grad * lax.rsqrt(moment_new)
    ratio = jnp.sqrt(lax.optimization_barrier(jnp.mean(update * update, axis=-1, keepdims=True))) / CLIP
    update = update / jnp.maximum(ratio, 1.0)
    scale = jnp.maximum(jnp.sqrt(lax.optimization_barrier(jnp.mean(param * param, axis=-1, keepdims=True))), FLOOR)
    return (moment_new, param - RHO * scale * update)

def reference(frames, cotangent, lengths, attn_in, attn_out, ffn_up, ffn_down, norm_params, skip_proj, in_rows, in_cols, out_rows, out_cols, up_rows, up_cols, down_rows, down_cols, skip_rows, skip_cols, norm_moment):
    params = (attn_in, attn_out, ffn_up, ffn_down, norm_params, skip_proj)
    flat_frames = frames.reshape(MICRO * BATCH, SEQ, D)
    flat_grads = cotangent.reshape(MICRO * BATCH, SEQ, D)
    flat_lengths = lengths.reshape(MICRO * BATCH)

    def one_item(totals, item):
        source, outer_grad, length = item
        valid_rows = (jnp.arange(SEQ) < length).astype(jnp.float32)[:, None]
        probe_add = jnp.zeros((SEQ, D), jnp.float32)

        def forward(weights_all, source_in, probe_in):
            return utterance(weights_all, source_in, probe_in, length)
        outputs, pullback = jax.vjp(forward, params, source, probe_add)
        param_grads, source_grad, probe_grad = pullback((outer_grad * valid_rows, jnp.zeros_like(outputs[1])))
        totals = jax.tree.map(jnp.add, totals, param_grads)
        return (totals, (outputs[0], outputs[1], source_grad, probe_grad))
    zeros_tree = jax.tree.map(jnp.zeros_like, params)
    totals, gathered = lax.scan(one_item, zeros_tree, (flat_frames, flat_grads, flat_lengths))
    shape = (MICRO, BATCH, SEQ, D)
    layer_outputs = jnp.stack([gathered[0].reshape(shape), gathered[1].reshape(shape)])
    input_grads = jnp.stack([gathered[2].reshape(shape), gathered[3].reshape(shape)])
    result_in = stacked_update(totals[0], attn_in, in_rows, in_cols)
    result_out = stacked_update(totals[1], attn_out, out_rows, out_cols)
    result_up = stacked_update(totals[2], ffn_up, up_rows, up_cols)
    result_down = stacked_update(totals[3], ffn_down, down_rows, down_cols)
    skip_rows_new, skip_cols_new, skip_new = factored(totals[5], skip_proj, skip_rows, skip_cols)
    moment_new, norms_new = unfactored(totals[4], norm_params, norm_moment)
    return (layer_outputs, input_grads, result_in[0], result_in[1], result_in[2], result_in[3], result_out[0], result_out[1], result_out[2], result_out[3], result_up[0], result_up[1], result_up[2], result_up[3], result_down[0], result_down[1], result_down[2], result_down[3], totals[5], skip_rows_new, skip_cols_new, skip_new, totals[4], moment_new, norms_new)
```

```python
from functools import partial

import jax
import jax.numpy as jnp
from jax import lax
from jax.sharding import PartitionSpec as P

HEADS = 16
STEP = 10


EPS = 1e-05
TINY = 1e-30
CLIP = 1.0
RHO = 0.5
FLOOR = 0.001
MASKED = -1e30
PRECISE = lax.Precision.HIGH
DECAY = 1.0 - STEP ** (-0.8)
NEAR = 4
PAD = 128


def place():
    me = lax.axis_index("dp")
    return me // NEAR, (me // 2) % 2, me % 2


def swap_core(block):
    return lax.ppermute(block, "section", [(0, 1), (1, 0)])


def swap_dp(block, mask):
    return lax.ppermute(block, "dp", [(i, i ^ mask) for i in range(lax.axis_size("dp"))])


def swap_split(block, mask_zero, mask_one):
    count = lax.axis_size("dp")
    masks = (mask_zero, mask_one)
    route = [(s * count + i, s * count + (i ^ masks[s])) for s in range(2) for i in range(count)]
    return lax.ppermute(block, ("section", "dp"), route)


class Lane:
    def __init__(self, depth):
        self.depth = depth
        self.given = []

    def send(self, block, move):
        if len(self.given) >= self.depth:
            block, _ = lax.optimization_barrier((block, self.given[-self.depth]))
        out = move(block)
        self.given.append(out)
        return out


def far_groups(count):
    return [[k * NEAR + low for k in range(count // NEAR)] for low in range(NEAR)]


def gather_shards(shard, lanes):
    count = lax.axis_size("dp")
    far = count // NEAR
    z, y, x = place()
    first = lax.axis_index("section") == 0
    if far > 4:
        column = lax.all_gather(shard, "dp", axis_index_groups=far_groups(count))
    else:
        column = jnp.zeros((far,) + shard.shape, shard.dtype)
        column = lax.dynamic_update_slice(column, shard[None], (z, 0, 0))
        found = lanes["z"].send(
            shard, lambda block: tuple(swap_dp(block, NEAR * k) for k in range(1, far))
        )
        for k in range(1, far):
            column = lax.dynamic_update_slice(column, found[k - 1][None], (z ^ k, 0, 0))
    from_x, from_y = lanes["xy"].send(column, lambda block: (swap_dp(block, 1), swap_dp(block, 2)))
    from_both = lanes["d"].send(
        jnp.where(first, from_x, from_y), lambda block: swap_split(block, 2, 1)
    )
    return (column, from_x, from_y, from_both)


def assemble(parts, low, high):
    z, y, x = place()
    column, from_x, from_y, from_both = [part[:, :, low:high] for part in parts]
    far, rows, width = column.shape
    whole = jnp.zeros((far, 2, 2, rows, width), column.dtype)
    whole = lax.dynamic_update_slice(whole, column[:, None, None], (0, y, x, 0, 0))
    whole = lax.dynamic_update_slice(whole, from_x[:, None, None], (0, y, 1 - x, 0, 0))
    whole = lax.dynamic_update_slice(whole, from_y[:, None, None], (0, 1 - y, x, 0, 0))
    whole = lax.dynamic_update_slice(whole, from_both[:, None, None], (0, 1 - y, 1 - x, 0, 0))
    own = whole.reshape(far * NEAR * rows, width)
    return (own, swap_core(own))


def combine(own, other, lanes):
    return own + lanes["c"].send(other, swap_core)


def spread(summed, lanes):
    count = lax.axis_size("dp")
    far = count // NEAR
    z, y, x = place()
    first = lax.axis_index("section") == 0
    rows, width = summed.shape[0] // count, summed.shape[1]
    blocks = summed.reshape(far, 2, 2, rows, width)

    def take(a, b):
        return lax.dynamic_slice(blocks, (0, a, b, 0, 0), (far, 1, 1, rows, width))[:, 0, 0]

    corner = lanes["d"].send(take(1 - y, 1 - x), lambda block: swap_split(block, 1, 2))
    to_x = take(y, 1 - x) + jnp.where(first, 0.0, corner)
    to_y = take(1 - y, x) + jnp.where(first, corner, 0.0)
    from_x, from_y = lanes["xy"].send(
        (to_x, to_y), lambda pair: (swap_dp(pair[0], 1), swap_dp(pair[1], 2))
    )
    column = take(y, x) + from_x + from_y
    if far > 4:
        return lax.psum_scatter(column, "dp", axis_index_groups=far_groups(count))

    def pick(k):
        return lax.dynamic_index_in_dim(column, z ^ k, 0, keepdims=False)

    found = lanes["z"].send(
        tuple(pick(k) for k in range(1, far)),
        lambda parts: tuple(swap_dp(part, NEAR * (k + 1)) for k, part in enumerate(parts)),
    )
    total = pick(0)
    for part in found:
        total = total + part
    return total


def hold(first, *rest):
    return lax.optimization_barrier((first, rest))[0]


def total_dp(values):
    mask = 1
    while mask < lax.axis_size("dp"):
        values = values + swap_dp(values, mask)
        mask *= 2
    return values


def by_layer(own, other, axis):
    first = lax.axis_index("section") == 0
    return jnp.where(
        first, jnp.concatenate([own, other], axis), jnp.concatenate([other, own], axis)
    )


def halves(block):
    half = block.shape[1] // 2
    section = lax.axis_index("section")
    own = lax.dynamic_slice_in_dim(block, section * half, half, 1)
    other = lax.dynamic_slice_in_dim(block, (1 - section) * half, half, 1)
    return (own, other)


def dot(left, right):
    return jnp.dot(left, right, precision=PRECISE)


def dot_t(left, right):
    return lax.dot_general(left, right, (((1,), (1,)), ((), ())), precision=PRECISE)


def t_dot(left, right):
    return lax.dot_general(left, right, (((0,), (0,)), ((), ())), precision=PRECISE)


def normalise(stream):
    centered = stream - jnp.mean(stream, axis=-1, keepdims=True)
    spread = jnp.mean(centered * centered, axis=-1, keepdims=True)
    inverse = lax.rsqrt(spread + EPS)
    return (centered * inverse, inverse)


def norm_backward(grad, unit, inverse, gain):
    scaled = grad * gain
    back = scaled - jnp.mean(scaled, axis=-1, keepdims=True)
    back = back - unit * jnp.mean(scaled * unit, axis=-1, keepdims=True)
    return (inverse * back, jnp.sum(grad * unit, axis=0), jnp.sum(grad, axis=0))


def heads_attention(projected, first_head, length, head_width):
    frame_count = projected.shape[0]
    head_count = projected.shape[1] // (3 * head_width)
    split = projected.reshape(frame_count, 3, head_count, head_width)
    scores = jnp.einsum("qhd,khd->hqk", split[:, 0], split[:, 1], precision=PRECISE)
    scores = scores * head_width ** (-0.5)
    positions = jnp.arange(frame_count)
    distance = jnp.abs(positions[:, None] - positions[None, :]).astype(jnp.float32)
    heads = (first_head + jnp.arange(head_count)).astype(jnp.float32)
    slopes = 2.0 ** (-8.0 * (heads + 1.0) / HEADS)
    scores = scores - slopes[:, None, None] * distance[None]
    scores = jnp.where((positions < length)[None, None, :], scores, MASKED)
    weighted = jnp.exp(scores - jnp.max(scores, axis=-1, keepdims=True))
    probability = weighted / jnp.sum(weighted, axis=-1, keepdims=True)
    context = jnp.einsum("hqk,khd->qhd", probability, split[:, 2], precision=PRECISE)
    return context.reshape(frame_count, head_count * head_width)


def attention_forward(stream, gain, shift, weights, length):
    in_own, in_other, out_own, out_other = weights
    section = lax.axis_index("section")
    unit, inverse = normalise(stream)
    normed = unit * gain + shift
    head_width = stream.shape[1] // HEADS
    half = HEADS // 2
    contexts = []
    pulls = []
    for w_in, first_head in ((in_own, section * half), (in_other, (1 - section) * half)):
        attend = partial(
            heads_attention, first_head=first_head, length=length, head_width=head_width
        )
        context, pull = jax.vjp(attend, dot(normed, w_in))
        contexts.append(context)
        pulls.append(pull)
    context = by_layer(contexts[0], contexts[1], 1)
    out = stream + by_layer(dot(context, out_own), dot(context, out_other), 1)
    return (out, (unit, inverse, gain, normed, context, pulls))


def attention_backward(grad, saved, weights, lanes):
    in_own, in_other, out_own, out_other = weights
    unit, inverse, gain, normed, context, pulls = saved
    grad_own, grad_other = halves(grad)
    out_grad = combine(t_dot(context, grad_own), t_dot(context, grad_other), lanes)
    context_grad = dot_t(grad_own, out_own) + dot_t(grad_other, out_other)
    back = [pull(part)[0] for pull, part in zip(pulls, halves(context_grad))]
    in_other_grad = t_dot(normed, back[1])
    in_grad = combine(t_dot(normed, back[0]), in_other_grad, lanes)
    back[0] = hold(back[0], in_other_grad)
    normed_grad = dot_t(back[0], in_own) + dot_t(back[1], in_other)
    stream_grad, gain_grad, shift_grad = norm_backward(normed_grad, unit, inverse, gain)
    grad = hold(grad + stream_grad, in_grad, out_grad)
    return (grad, spread(out_grad, lanes), spread(in_grad, lanes), gain_grad, shift_grad)


def feed_forward(stream, gain, shift, weights):
    up_own, up_other, down_own, down_other = weights
    unit, inverse = normalise(stream)
    normed = unit * gain + shift
    inner = (dot(normed, up_own), dot(normed, up_other))
    hidden = [jax.nn.gelu(part, approximate=False) for part in inner]
    out = stream + dot(hidden[0], down_own) + dot(hidden[1], down_other)
    return (out, (unit, inverse, gain, normed, inner, hidden))


def gelu_slope(value):
    bell = jnp.exp(-0.5 * value * value) * 0.3989422804014327
    return 0.5 * (1.0 + lax.erf(value * 0.7071067811865476)) + value * bell


def feed_backward(grad, saved, weights, lanes):
    up_own, up_other, down_own, down_other = weights
    unit, inverse, gain, normed, inner, hidden = saved
    down_other_grad = t_dot(hidden[1], grad)
    down_grad = combine(t_dot(hidden[0], grad), down_other_grad, lanes)
    held = hold(grad, down_other_grad)
    back_other = dot_t(held, down_other) * gelu_slope(inner[1])
    up_other_grad = t_dot(normed, back_other)
    held = hold(held, up_other_grad)
    back_own = dot_t(held, down_own) * gelu_slope(inner[0])
    up_grad = combine(t_dot(normed, back_own), up_other_grad, lanes)
    normed_grad = dot_t(back_own, up_own) + dot_t(back_other, up_other)
    stream_grad, gain_grad, shift_grad = norm_backward(normed_grad, unit, inverse, gain)
    grad = hold(grad + stream_grad, down_grad, up_grad)
    return (grad, spread(down_grad, lanes), spread(up_grad, lanes), gain_grad, shift_grad)


def local_moments(grad, rows_old, weight):
    squared = grad * grad + TINY
    rows_new = DECAY * rows_old + (1.0 - DECAY) * jnp.mean(squared, axis=1)
    scaled = jnp.sum(grad * grad / rows_new[:, None], axis=0)
    pair = jnp.stack([jnp.sum(rows_new), jnp.sum(weight * weight)])
    return (rows_new, [jnp.sum(squared, axis=0), scaled, pair])


def finish(grad, weight, rows_new, cols_old, totals, total_rows):
    column_total, scaled_total, pair = totals
    cols_new = DECAY * cols_old + (1.0 - DECAY) * (column_total / total_rows)
    rows_mean = pair[0] / total_rows
    second = rows_new[:, None] * cols_new[None, :] / rows_mean
    update = grad * lax.rsqrt(second)
    count = total_rows * grad.shape[1]
    ratio = jnp.sqrt(rows_mean * jnp.sum(scaled_total / cols_new) / count) / CLIP
    scale = jnp.maximum(jnp.sqrt(pair[1] / count), FLOOR)
    return (cols_new, weight - RHO * scale * (update / jnp.maximum(ratio, 1.0)))


def on_device(
    frames,
    cotangent,
    lengths,
    attn_in,
    attn_out,
    ffn_up,
    ffn_down,
    norm_params,
    skip_proj,
    in_rows,
    in_cols,
    out_rows,
    out_cols,
    up_rows,
    up_cols,
    down_rows,
    down_cols,
    skip_rows,
    skip_cols,
    norm_moment,
):
    section = lax.axis_index("section")
    me = lax.axis_index("dp")
    data_size = lax.axis_size("dp")
    first = section == 0
    frame_count, model_width = frames.shape[2], frames.shape[3]
    width = model_width // 2
    share = attn_in.shape[1]
    ffn_share = ffn_down.shape[1]
    source = lax.dynamic_index_in_dim(frames, section, 0, keepdims=False)[0]
    length = lax.dynamic_index_in_dim(lengths, section, 0, keepdims=False)[0]
    valid_rows = (jnp.arange(frame_count) < length).astype(jnp.float32)[:, None]
    outer = lax.dynamic_index_in_dim(cotangent, section, 0, keepdims=False)[0] * valid_rows

    def attn_half(s):
        heads_in = attn_in[0].reshape(share, 3, 2, width)
        inner = lax.dynamic_index_in_dim(heads_in, s, 2, keepdims=False).reshape(share, 3 * width)
        return jnp.concatenate(
            [inner, lax.dynamic_slice_in_dim(attn_out[0], s * width, width, 1)], 1
        )

    def up_half(s):
        hidden_cols = ffn_up[0].reshape(share, data_size, 2, ffn_share // 2)
        return lax.dynamic_index_in_dim(hidden_cols, s, 2, keepdims=False).reshape(share, -1)

    def down_half(s):
        return lax.dynamic_slice_in_dim(ffn_down[0], s * (ffn_share // 2), ffn_share // 2, 0)

    def by_owner(half):
        kept = half(section)
        given = swap_core(half(1 - section))
        return (jnp.where(first, kept, given), jnp.where(first, given, kept))

    attn_zero, attn_one = by_owner(attn_half)
    up_zero, up_one = by_owner(up_half)
    down_zero, down_one = by_owner(down_half)
    norm_shard = jnp.pad(norm_params[0].T, ((0, 0), (0, PAD - norm_params.shape[1])))

    lanes = {"z": Lane(1), "xy": Lane(1), "d": Lane(1)}
    parts = gather_shards(jnp.concatenate([attn_zero, norm_shard], 1), lanes)
    attn_zero_full = assemble(parts, 0, 3 * width) + assemble(parts, 3 * width, 4 * width)
    norms = [full[:, :4].T for full in assemble(parts, 4 * width, 4 * width + PAD)]
    norm_zero = jnp.where(first, norms[0], norms[1])
    norm_one = jnp.where(first, norms[1], norms[0])
    ffn_one_full = assemble(gather_shards(up_one, lanes), 0, up_one.shape[1]) + assemble(
        gather_shards(down_one, lanes), 0, model_width
    )
    skip_full = assemble(gather_shards(skip_proj, lanes), 0, model_width)
    parts = gather_shards(attn_one, lanes)
    attn_one_full = assemble(parts, 0, 3 * width) + assemble(parts, 3 * width, 4 * width)
    ffn_zero_full = assemble(gather_shards(up_zero, lanes), 0, up_zero.shape[1]) + assemble(
        gather_shards(down_zero, lanes), 0, model_width
    )

    after_attn, saved_a0 = attention_forward(
        source, norm_zero[0], norm_zero[1], attn_zero_full, length
    )
    twelve, saved_f1 = feed_forward(after_attn, norm_one[2], norm_one[3], ffn_one_full)
    joined_own = jnp.where(first, twelve, source)
    joined_other = jnp.where(first, source, twelve)
    joined = dot(joined_own, skip_full[0]) + dot(joined_other, skip_full[1])
    middle, saved_a1 = attention_forward(
        joined, norm_one[0], norm_one[1], attn_one_full, length
    )
    thirteen, saved_f0 = feed_forward(middle, norm_zero[2], norm_zero[3], ffn_zero_full)

    lanes = {"z": Lane(1), "xy": Lane(1), "d": Lane(1), "c": Lane(2)}
    grad, down_zero_s, up_zero_s, g02, g03 = feed_backward(outer, saved_f0, ffn_zero_full, lanes)
    grad, out_one_s, in_one_s, g10, g11 = attention_backward(
        grad, saved_a1, attn_one_full, lanes
    )
    skip_sum = combine(t_dot(joined_own, grad), t_dot(joined_other, grad), lanes)
    skip_grad = spread(skip_sum, lanes)
    back_own = dot_t(grad, skip_full[0])
    back_other = dot_t(grad, skip_full[1])
    frames_grad = jnp.where(first, back_other, back_own)
    grad = hold(jnp.where(first, back_own, back_other), skip_sum)
    grad, down_one_s, up_one_s, g12, g13 = feed_backward(grad, saved_f1, ffn_one_full, lanes)
    after_attn_grad = grad
    grad, out_zero_s, in_zero_s, g00, g01 = attention_backward(
        grad, saved_a0, attn_zero_full, lanes
    )
    frames_grad = frames_grad + grad

    def to_owner(zero, one):
        kept = jnp.where(first, zero, one)
        given = swap_core(jnp.where(first, one, zero))
        return (jnp.where(first, kept, given), jnp.where(first, given, kept))

    def regroup(pair, groups):
        parts = [part.reshape(part.shape[0], groups, -1) for part in pair]
        return jnp.stack(parts, 2).reshape(parts[0].shape[0], -1)

    shares = [
        regroup(to_owner(in_zero_s, in_one_s), 3),
        regroup(to_owner(out_zero_s, out_one_s), 1),
        regroup(to_owner(up_zero_s, up_one_s), data_size),
        jnp.concatenate(to_owner(down_zero_s, down_one_s), 0),
    ]

    norm_grads = total_dp(jnp.stack([g00, g01, g02, g03, g10, g11, g12, g13]))
    norm_grads = (norm_grads + swap_core(norm_grads)).reshape(2, 4, model_width)
    norm_share = lax.dynamic_slice(norm_grads, (section, 0, me * share), (1, 4, share))[0]

    current = [attn_in[0], attn_out[0], ffn_up[0], ffn_down[0]]
    rows_old = [in_rows[0], out_rows[0], up_rows[0], down_rows[0]]
    cols_old = [in_cols[0], out_cols[0], up_cols[0], down_cols[0]]
    moments = [local_moments(g, r, w) for g, r, w in zip(shares, rows_old, current)]
    skip_rows_new, skip_local = local_moments(skip_grad, skip_rows, skip_proj)
    norm_moment_new = DECAY * norm_moment[0] + (1.0 - DECAY) * (norm_share * norm_share + TINY)
    norm_raw = norm_share * lax.rsqrt(norm_moment_new)
    norm_sums = [
        jnp.sum(norm_raw * norm_raw, axis=-1),
        jnp.sum(norm_params[0] * norm_params[0], axis=-1),
    ]
    vectors = skip_local + [v for _, local in moments for v in local] + norm_sums
    sizes = [v.shape[0] for v in vectors]
    packed = jnp.concatenate(vectors)
    packed = total_dp(jnp.pad(packed, (0, -packed.shape[0] % PAD)))
    skip_size = sum(sizes[:3])
    skip_totals = packed[:skip_size] + swap_core(packed[:skip_size])
    offsets = [sum(sizes[:k]) for k in range(len(sizes))]
    totals = [packed[at : at + size] for at, size in zip(offsets, sizes)]
    updated = [
        finish(
            shares[k],
            current[k],
            moments[k][0],
            cols_old[k],
            totals[3 + 3 * k : 6 + 3 * k],
            shares[k].shape[0] * data_size,
        )
        for k in range(4)
    ]
    skip_cols_new, skip_new = finish(
        skip_grad,
        skip_proj,
        skip_rows_new,
        skip_cols,
        [skip_totals[at : at + size] for at, size in zip(offsets[:3], sizes[:3])],
        skip_grad.shape[0] * data_size * 2,
    )
    norm_ratio = jnp.sqrt(totals[15] / model_width) / CLIP
    norm_scale = jnp.maximum(jnp.sqrt(totals[16] / model_width), FLOOR)
    norms_new = norm_params[0] - RHO * norm_scale[:, None] * (
        norm_raw / jnp.maximum(norm_ratio, 1.0)[:, None]
    )

    def both_micro(zero, one):
        kept = jnp.where(first, zero, one)
        given = swap_core(jnp.where(first, one, zero))
        pair = jnp.where(first, jnp.stack([kept, given]), jnp.stack([given, kept]))
        return pair[None, :, None]

    layer_outputs = both_micro(thirteen, twelve)
    input_grads = both_micro(frames_grad, after_attn_grad)
    return (
        layer_outputs,
        input_grads,
        shares[0][None],
        moments[0][0][None],
        updated[0][0][None],
        updated[0][1][None],
        shares[1][None],
        moments[1][0][None],
        updated[1][0][None],
        updated[1][1][None],
        shares[2][None],
        moments[2][0][None],
        updated[2][0][None],
        updated[2][1][None],
        shares[3][None],
        moments[3][0][None],
        updated[3][0][None],
        updated[3][1][None],
        skip_grad,
        skip_rows_new,
        skip_cols_new,
        skip_new,
        norm_share[None],
        norm_moment_new[None],
        norms_new[None],
    )


def solution(mesh):
    return jax.shard_map(
        on_device,
        mesh=mesh,
        in_specs=(
            P(None, "dp", None, None),
            P(None, "dp", None, None),
            P(None, "dp"),
            P("section", "dp", None),
            P("section", "dp", None),
            P("section", "dp", None),
            P("section", "dp", None),
            P("section", None, "dp"),
            P(("section", "dp"), None),
            P("section", "dp"),
            P("section", None),
            P("section", "dp"),
            P("section", None),
            P("section", "dp"),
            P("section", None),
            P("section", "dp"),
            P("section", None),
            P(("section", "dp")),
            P(),
            P("section", None, "dp"),
        ),
        out_specs=(
            P("section", None, "dp", None, None),
            P("section", None, "dp", None, None),
            P("section", "dp", None),
            P("section", "dp"),
            P("section", None),
            P("section", "dp", None),
            P("section", "dp", None),
            P("section", "dp"),
            P("section", None),
            P("section", "dp", None),
            P("section", "dp", None),
            P("section", "dp"),
            P("section", None),
            P("section", "dp", None),
            P("section", "dp", None),
            P("section", "dp"),
            P("section", None),
            P("section", "dp", None),
            P(("section", "dp"), None),
            P(("section", "dp")),
            P(),
            P(("section", "dp"), None),
            P("section", None, "dp"),
            P("section", None, "dp"),
            P("section", None, "dp"),
        ),
        check_vma=False,
    )
```

```python
import math
from functools import partial

import jax
import jax.numpy as jnp
from jax import lax
from jax.experimental import pallas as pl
from jax.experimental.pallas import tpu as pltpu
from jax.sharding import PartitionSpec as P

HEADS = 16
STEP = 10


EPS = 1e-05
TINY = 1e-30
CLIP = 1.0
RHO = 0.5
FLOOR = 0.001
MASKED = -1e30
DECAY = 1.0 - STEP ** (-0.8)
PAD = 128
DIRECT = 16


def swap_core(block):
    return lax.ppermute(block, "section", [(0, 1), (1, 0)])


def swap_dp(block, mask):
    return lax.ppermute(block, "dp", [(i, i ^ mask) for i in range(lax.axis_size("dp"))])


def swap_split(block, mask_zero, mask_one):
    count = lax.axis_size("dp")
    masks = (mask_zero, mask_one)
    route = [(s * count + i, s * count + (i ^ masks[s])) for s in range(2) for i in range(count)]
    return lax.ppermute(block, ("section", "dp"), route)


def hold(first, *rest):
    return lax.optimization_barrier((first, rest))[0] if rest else first


class Line:
    def __init__(self):
        self.waits = ()

    def run(self, kernel, left, *rest, **how):
        if isinstance(left, tuple):
            left = (hold(left[0], *self.waits),) + left[1:]
        else:
            left = hold(left, *self.waits)
        out = kernel(left, *rest, **how)
        self.waits = (out,)
        return out

    def need(self, *arrays):
        self.waits += arrays


class Gather:
    def __init__(self, shards):
        self.shards = shards
        self.columns, self.sides, self.wholes = [], [], []
        self.over = ()
        self.mine = None
        if lax.axis_size("dp") != DIRECT:
            for shard in shards:
                whole = lax.all_gather(shard, "dp", axis=0, tiled=True)
                self.wholes.append((whole, swap_core(whole)))


    def turn(self, *needs):
        if lax.axis_size("dp") != DIRECT:
            return
        me = lax.axis_index("dp")
        first = lax.axis_index("section") == 0
        at = len(self.columns)
        over = self.over + needs
        sent = {}
        if at < len(self.shards):
            rows, width = self.shards[at].shape
            shard = hold(self.shards[at], *over)
            found = swap_dp(shard, 4)
            two = interleave(shard[None], found[None], (me // 4) % 2).reshape(2 * rows, width)
            sent["z"] = swap_dp(two, 8)
        if 0 <= at - 1 < len(self.shards):
            column = hold(self.columns[at - 1], *over)
            sent["xy"] = (swap_dp(column, 1), swap_dp(column, 2))
        if 0 <= at - 2 < len(self.shards):
            from_x, from_y = self.sides[at - 1]
            carried = hold(jnp.where(first, from_x, from_y), *over)
            sent["both"] = swap_split(carried, 2, 1)
        if self.mine is not None:
            sent["core"] = swap_core(hold(self.mine, *over))
        sent = lax.optimization_barrier(sent)
        if "core" in sent:
            self.wholes.append((self.mine, sent["core"]))
        self.mine = None
        new_column = None
        if "z" in sent:
            new_column = interleave(two[None], sent["z"][None], me // 8).reshape(4, rows, width)
        if "both" in sent:
            whole = place_four((self.columns[at - 2], from_x, from_y, sent["both"]))
            self.mine = whole.reshape(-1, whole.shape[-1])
        self.columns.append(new_column)
        self.sides.append(sent.get("xy"))
        self.over = tuple(jax.tree.leaves(sent))


class Sums:
    def __init__(self):
        self.over = ()
        self.sent = {}
        self.kept = (None,) * 4
        self.corner = None
        self.column = None
        self.pair = None
        self.totals = []

    def close(self, summed=None):
        sent, summed = lax.optimization_barrier((self.sent, summed))
        take, take_last, keep, keep_near = self.kept
        self.corner = (take, sent["corner"]) if "corner" in sent else None
        self.column = (take_last,) + sent["xy"] if "xy" in sent else None
        self.pair = keep + sent["far"] if "far" in sent else None
        if "near" in sent:
            self.totals.append(keep_near + sent["near"])
        self.over = tuple(jax.tree.leaves(sent))
        self.sent = {}
        return summed

    def turn(self, summed=None):
        if lax.axis_size("dp") != DIRECT:
            if summed is not None:
                self.totals.append(
                    lax.psum_scatter(summed, "dp", scatter_dimension=0, tiled=True)
                )
            return ()
        me = lax.axis_index("dp")
        y, x = (me // 2) % 2, me % 2
        first = lax.axis_index("section") == 0
        summed = self.close(summed)
        sent, operands = {}, ()

        def split(part, bit):
            keep = lax.dynamic_index_in_dim(part, bit, 0, keepdims=False)
            return keep, lax.dynamic_index_in_dim(part, 1 - bit, 0, keepdims=False)

        if summed is not None:
            rows, width = summed.shape[0] // DIRECT, summed.shape[1]
            blocks = summed.reshape(4, 2, 2, rows, width)

            def take(a, b):
                part = lax.dynamic_slice(blocks, (0, a, b, 0, 0), (4, 1, 1, rows, width))
                return part[:, 0, 0]

            give = hold(take(1 - y, 1 - x), *self.over)
            sent["corner"] = swap_split(give, 1, 2)
            operands += (give,)
        if self.corner is not None:
            take_last, found = self.corner
            to_x = take_last(y, 1 - x) + jnp.where(first, 0.0, found)
            to_y = take_last(1 - y, x) + jnp.where(first, found, 0.0)
            to_x, to_y = hold((to_x, to_y), *self.over)
            sent["xy"] = (swap_dp(to_x, 1), swap_dp(to_y, 2))
            operands += (to_x, to_y)
        if self.column is not None:
            take_old, from_x, from_y = self.column
            part = take_old(y, x) + from_x + from_y
            part = part.reshape((2, 2) + part.shape[1:])
            keep, give = split(part, me // 8)
            give = hold(give, *self.over)
            operands += (give,)
            sent["far"] = swap_dp(give, 8)
        if self.pair is not None:
            keep_near, give = split(self.pair, (me // 4) % 2)
            give = hold(give, *self.over)
            operands += (give,)
            sent["near"] = swap_dp(give, 4)
        self.sent = sent
        self.kept = (
            take if "corner" in sent else None,
            take_last if "xy" in sent else None,
            keep if "far" in sent else None,
            keep_near if "near" in sent else None,
        )
        return self.over + operands


def total_dp(values):
    mask = 1
    while mask < lax.axis_size("dp"):
        values = values + swap_dp(values, mask)
        mask *= 2
    return values


TILE = 256


def parts_of(value):
    high = value.astype(jnp.bfloat16)
    return high, (value - high.astype(jnp.float32)).astype(jnp.bfloat16)


def product(left, right, dims):
    total = None
    for a, b in ((left[0], right[1]), (left[1], right[0]), (left[0], right[0])):
        one = lax.dot_general(a, b, (dims, ((), ())), preferred_element_type=jnp.float32)
        total = one if total is None else total + one
    return total


PLAIN = ((1,), (0,))
FLIPPED = ((1,), (1,))
GRADS = ((0,), (0,))


def kernel_call(body, grid, in_specs, out_shape, out_spec, scratch, depth, prefetch=1):
    return pl.pallas_call(
        body,
        out_shape=jax.ShapeDtypeStruct(out_shape, jnp.float32),
        grid_spec=pltpu.PrefetchScalarGridSpec(
            num_scalar_prefetch=prefetch,
            grid=grid,
            in_specs=in_specs,
            out_specs=out_spec,
            scratch_shapes=scratch,
        ),
        compiler_params=pltpu.CompilerParams(vmem_limit_bytes=52 * 2**20),
        cost_estimate=pl.CostEstimate(
            flops=depth * math.prod(out_shape) // 4, bytes_accessed=0, transcendentals=0
        ),
    )


def section_index():
    return lax.axis_index("section").astype(jnp.int32)[None]


def wide_body(where, left, own, other, *rest, dims, scaled):
    scale = rest[0] if scaled else None
    out, high, low = rest[-3:]

    @pl.when((pl.program_id(0) == 0) & (pl.program_id(1) == 0))
    def _():
        high[...], low[...] = parts_of(left[...])

    def one(right):
        found = product((high[...], low[...]), parts_of(right[...]), dims)
        out[...] = found * scale[...] if scaled else found

    pl.when(pl.program_id(0) == 0)(lambda: one(own))
    pl.when(pl.program_id(0) == 1)(lambda: one(other))


def wide(left, own, other, flipped=False, by_section=False, scale=None, window=None):
    rows, depth = left.shape
    start, columns = window or (0, own.shape[1])
    width = own.shape[0] if flipped else columns
    tile = math.gcd(TILE, width)
    tiles = width // tile
    at = start // columns if flipped else start // tile

    def right(half):
        def index(h, j, where):
            stay = tiles - 1 if half == 0 else 0
            k = jnp.where(h == half, j, stay)
            return (k, at) if flipped else (0, at + k)

        return pl.BlockSpec((tile, depth) if flipped else (depth, tile), index)

    def out_index(h, j, where):
        half = h + where[0] - 2 * h * where[0] if by_section else h
        return (0, half * tiles + j)

    out_spec = pl.BlockSpec((rows, tile), out_index)
    in_specs = [pl.BlockSpec((rows, depth), lambda h, j, where: (0, 0)), right(0), right(1)]
    call = kernel_call(
        partial(wide_body, dims=FLIPPED if flipped else PLAIN, scaled=scale is not None),
        (2, tiles),
        in_specs + ([] if scale is None else [out_spec]),
        (rows, 2 * width),
        out_spec,
        [pltpu.VMEM((rows, depth), jnp.bfloat16)] * 2,
        depth,
    )
    return call(section_index(), left, own, other, *([] if scale is None else [scale]))


def both_body(where, left_own, left_other, own, other, out, *scratch, dims):
    @pl.when(pl.program_id(0) == 0)
    def _():
        scratch[0][...], scratch[1][...] = parts_of(left_own[...])
        scratch[2][...], scratch[3][...] = parts_of(left_other[...])

    found = product((scratch[0][...], scratch[1][...]), parts_of(own[...]), dims)
    out[...] = found + product((scratch[2][...], scratch[3][...]), parts_of(other[...]), dims)


def both(left, own, other, flipped=False, window=None, by_section=False):
    lefts = left if isinstance(left, tuple) else (left, left)
    split = not isinstance(left, tuple)
    rows, depth = lefts[0].shape
    depth = depth // 2 if split else depth
    start, columns = window or (0, own.shape[1])
    width = own.shape[0] if flipped else columns
    tile = math.gcd(TILE, width)
    at = start // columns if flipped else start // tile

    def left_spec(half):
        def index(j, where):
            if not split:
                return (0, 0)
            return (0, (where[0] if half == 0 else 1 - where[0]) if by_section else half)

        return pl.BlockSpec((rows, depth), index)

    def right_index(j, where):
        return (j, at) if flipped else (0, at + j)

    right = pl.BlockSpec((tile, depth) if flipped else (depth, tile), right_index)
    call = kernel_call(
        partial(both_body, dims=FLIPPED if flipped else PLAIN),
        (width // tile,),
        [left_spec(0), left_spec(1), right, right],
        (rows, width),
        pl.BlockSpec((rows, tile), lambda j, where: (0, j)),
        [pltpu.VMEM((rows, depth), jnp.bfloat16)] * 4,
        2 * depth,
    )
    return call(section_index(), lefts[0], lefts[1], own, other)


def grads_body(where, left, right, *rest, added):
    more = rest[0] if added else None
    out, high, low = rest[-3:]

    @pl.when(pl.program_id(0) == 0)
    def _():
        high[...], low[...] = parts_of(right[...])

    found = product(parts_of(left[...]), (high[...], low[...]), GRADS)
    out[...] = found + more[...] if added else found


def grads(left, right, left_half=None, right_half=None, by_section=False, more=None):
    rows = left.shape[0]
    depth = left.shape[1] if left_half is None else left.shape[1] // 2
    width = right.shape[1] if right_half is None else right.shape[1] // 2
    tile = math.gcd(TILE, depth)
    tiles = depth // tile
    first = 0 if left_half is None else left_half * tiles

    def right_index(k, where):
        if right_half is None:
            return (0, 0)
        if by_section:
            return (0, where[0] if right_half == 0 else 1 - where[0])
        return (0, right_half)

    out_spec = pl.BlockSpec((tile, width), lambda k, where: (k, 0))
    in_specs = [
        pl.BlockSpec((rows, tile), lambda k, where: (0, first + k)),
        pl.BlockSpec((rows, width), right_index),
    ]
    call = kernel_call(
        partial(grads_body, added=more is not None),
        (tiles,),
        in_specs + ([] if more is None else [out_spec]),
        (depth, width),
        out_spec,
        [pltpu.VMEM((rows, width), jnp.bfloat16)] * 2,
        rows,
    )
    return call(section_index(), left, right, *([] if more is None else [more]))


def grads_pair_body(where, left, right, left_out, right_out, *rest, added):
    more = rest[0] if added else None
    out, high, low, high_out, low_out = rest[-5:]

    @pl.when(pl.program_id(0) == 0)
    def _():
        high[...], low[...] = parts_of(right[...])
        high_out[...], low_out[...] = parts_of(right_out[...])

    cut = right.shape[1]
    found = product(parts_of(left[...]), (high[...], low[...]), GRADS)
    out[:, :cut] = found + more[:, :cut] if added else found
    found = product(parts_of(left_out[...]), (high_out[...], low_out[...]), GRADS)
    out[:, cut:] = found + more[:, cut:] if added else found


def grads_pair(left, right, left_out, right_out, half, more=None):
    rows, depth = left.shape
    width, width_out = right.shape[1] // 2, right_out.shape[1] // 2
    tile = math.gcd(TILE, depth)
    out_spec = pl.BlockSpec((tile, width + width_out), lambda k, where: (k, 0))
    left_spec = pl.BlockSpec((rows, tile), lambda k, where: (0, k))

    def by_section(k, where):
        return (0, where[0] if half == 0 else 1 - where[0])

    in_specs = [
        left_spec,
        pl.BlockSpec((rows, width), lambda k, where: (0, half)),
        left_spec,
        pl.BlockSpec((rows, width_out), by_section),
    ]
    call = kernel_call(
        partial(grads_pair_body, added=more is not None),
        (depth // tile,),
        in_specs + ([] if more is None else [out_spec]),
        (depth, width + width_out),
        out_spec,
        [pltpu.VMEM((rows, width), jnp.bfloat16)] * 2
        + [pltpu.VMEM((rows, width_out), jnp.bfloat16)] * 2,
        rows,
    )
    return call(
        section_index(), left, right, left_out, right_out, *([] if more is None else [more])
    )


def weigh(where, slopes, query, keys, head):
    rows, lanes = query.shape
    scores = product(parts_of(query), keys, FLIPPED) * (lanes // 2) ** (-0.5)
    queries = lax.broadcasted_iota(jnp.int32, (rows, rows), 0)
    positions = lax.broadcasted_iota(jnp.int32, (rows, rows), 1)
    distance = jnp.abs(queries - positions).astype(jnp.float32)
    scores = scores - slopes[head] * distance
    scores = jnp.where(positions < where[1], scores, MASKED)
    weighted = jnp.exp(scores - jnp.max(scores, axis=-1, keepdims=True))
    return weighted, 1.0 / jnp.sum(weighted, axis=-1, keepdims=True)


def of_head(block, which):
    lanes = lax.broadcasted_iota(jnp.int32, block.shape, 1)
    half = block.shape[1] // 2
    mine = lanes < half if which == 0 else lanes >= half
    return jnp.where(mine, block, 0.0), mine


def attend_body(where, slopes, projected, out):
    lanes = out.shape[1]
    query, key, value = [projected[:, k * lanes : (k + 1) * lanes] for k in range(3)]
    keys, values = parts_of(key), parts_of(value)
    found = []
    for which in range(2):
        mine_query, mine = of_head(query, which)
        weighted, scale = weigh(where, slopes, mine_query, keys, 2 * pl.program_id(0) + which)
        found.append(product(parts_of(weighted), values, PLAIN) * scale)
    out[...] = jnp.where(mine, found[1], found[0])


def attend_back_body(where, slopes, projected, grad, out):
    lanes = grad.shape[1]
    query, key, value = [projected[:, k * lanes : (k + 1) * lanes] for k in range(3)]
    queries, keys, values = parts_of(query), parts_of(key), parts_of(value)
    grad_parts = parts_of(grad[...])
    found = []
    for which in range(2):
        mine_query, mine = of_head(query, which)
        weighted, scale = weigh(where, slopes, mine_query, keys, 2 * pl.program_id(0) + which)
        probability = weighted * scale
        mine_grad, _ = of_head(grad[...], which)
        back = product(parts_of(mine_grad), values, FLIPPED)
        back = probability * (back - jnp.sum(probability * back, axis=-1, keepdims=True))
        back = parts_of(back * (lanes // 2) ** (-0.5))
        found.append(
            (
                product(back, keys, PLAIN),
                product(back, queries, GRADS),
                product(parts_of(probability), grad_parts, GRADS),
            )
        )
    for k in range(3):
        out[:, k * lanes : (k + 1) * lanes] = jnp.where(mine, found[1][k], found[0][k])


def head_pairs(body, projected, length, grad=None):
    rows = projected.shape[0]
    pairs = HEADS // 2
    half = pairs // 2
    lanes = projected.shape[1] // (3 * pairs)
    section = lax.axis_index("section")
    ids = jnp.stack([section, 1 - section])[:, None] * (HEADS // 2) + jnp.arange(HEADS // 2)
    slopes = 2.0 ** (-8.0 * (ids.reshape(-1).astype(jnp.float32) + 1.0) / HEADS)

    def in_place(p, where, slopes):
        own = p // half
        return (0, (own + where[0] - 2 * own * where[0]) * half + p % half)

    wide_spec = pl.BlockSpec((rows, 3 * lanes), lambda p, where, slopes: (0, p))
    one_spec = pl.BlockSpec((rows, lanes), in_place)
    call = kernel_call(
        body,
        (pairs,),
        [wide_spec] if grad is None else [wide_spec, one_spec],
        (rows, lanes * pairs) if grad is None else projected.shape,
        one_spec if grad is None else wide_spec,
        [],
        rows,
        prefetch=2,
    )
    where = jnp.stack([section.astype(jnp.int32), length.astype(jnp.int32)])
    return call(where, slopes, projected, *([] if grad is None else [grad]))


def attend(projected, length):
    return head_pairs(attend_body, projected, length)


def attend_back(projected, grad, length):
    return head_pairs(attend_back_body, projected, length, grad)


def interleave_body(where, mine, given, out):
    @pl.when(pl.program_id(1) == 0)
    def _():
        out[0, 0] = mine[0]

    @pl.when(pl.program_id(1) == 1)
    def _():
        out[0, 0] = given[0]


def interleave(mine, given, bit):
    count, rows, width = mine.shape
    block = pl.BlockSpec((1, rows, width), lambda a, k, where: (a, 0, 0))
    out_spec = pl.BlockSpec(
        (1, 1, rows, width), lambda a, k, where: (a, where[0] + k - 2 * k * where[0], 0, 0)
    )
    call = kernel_call(
        interleave_body, (count, 2), [block, block], (count, 2, rows, width), out_spec, [], 0
    )
    return call(bit.astype(jnp.int32)[None], mine, given)


def place_body(where, own, from_x, from_y, from_both, out):
    for k, part in enumerate((own, from_x, from_y, from_both)):

        @pl.when(pl.program_id(0) == k)
        def _():
            out[0, 0, 0] = part[0]


def place_four(parts):
    count, rows, width = parts[0].shape
    me = lax.axis_index("dp")

    def part_spec(which):
        def index(k, a, where):
            return (jnp.where(k == which, a, jnp.where(k < which, 0, count - 1)), 0, 0)

        return pl.BlockSpec((1, rows, width), index)

    def out_index(k, a, where):
        y, x = k // 2, k % 2
        return (a, where[0] + y - 2 * y * where[0], where[1] + x - 2 * x * where[1], 0, 0)

    call = kernel_call(
        place_body,
        (4, count),
        [part_spec(which) for which in range(4)],
        (count, 2, 2, rows, width),
        pl.BlockSpec((1, 1, 1, rows, width), out_index),
        [],
        0,
    )
    return call(jnp.stack([(me // 2) % 2, me % 2]).astype(jnp.int32), *parts)


def normalise(stream):
    centered = stream - jnp.mean(stream, axis=-1, keepdims=True)
    spread = jnp.mean(centered * centered, axis=-1, keepdims=True)
    inverse = lax.rsqrt(spread + EPS)
    return (centered * inverse, inverse)


def norm_backward(grad, unit, inverse, gain):
    scaled = grad * gain
    back = scaled - jnp.mean(scaled, axis=-1, keepdims=True)
    back = back - unit * jnp.mean(scaled * unit, axis=-1, keepdims=True)
    return (inverse * back, jnp.sum(grad * unit, axis=0), jnp.sum(grad, axis=0))


def windows(stream):
    half = stream.shape[1] // 2
    return (0, 3 * half), (3 * half, half)


def attention_forward(stream, gain, shift, weights, length, line):
    window_in, window_out = windows(stream)
    unit, inverse = normalise(stream)
    normed = unit * gain + shift
    projected = line.run(wide, normed, *weights, window=window_in)
    context = line.run(attend, projected, length)
    out = stream + line.run(wide, context, *weights, window=window_out, by_section=True)
    return (out, (unit, inverse, gain, normed, projected, context))


def attention_backward(grad, saved, weights, length, line, send, under_way):
    unit, inverse, gain, normed, projected, context = saved
    window_in, window_out = windows(grad)
    back = line.run(both, grad, *weights, flipped=True, window=window_out, by_section=True)
    back = line.run(lambda g: attend_back(projected, g, length), back)
    line.need(*under_way())
    given = swap_core(line.run(grads_pair, normed, back, context, grad, 1))
    normed_grad = line.run(both, back, *weights, flipped=True, window=window_in)
    send(line.run(grads_pair, normed, back, context, grad, 0, more=given))
    stream_grad, gain_grad, shift_grad = norm_backward(normed_grad, unit, inverse, gain)
    return (grad + stream_grad, gain_grad, shift_grad)


def feed_forward(stream, gain, shift, weights, line):
    up_own, up_other, down_own, down_other = weights
    unit, inverse = normalise(stream)
    normed = unit * gain + shift
    inner = line.run(wide, normed, up_own, up_other)
    bell = jnp.exp(-0.5 * inner * inner) * 0.3989422804014327
    below = 0.5 * (1.0 + lax.erf(inner * 0.7071067811865476))
    hidden = inner * below
    slope = below + inner * bell

    def finish():
        return stream + line.run(both, hidden, down_own, down_other)

    return (finish, (unit, inverse, gain, normed, hidden, slope))


def feed_backward(grad, saved, weights, line, between, send_down, send_up):
    up_own, up_other, down_own, down_other = weights
    unit, inverse, gain, normed, hidden, slope = saved
    down_given = swap_core(line.run(grads, hidden, grad, left_half=1))
    between(0)
    back = line.run(wide, grad, down_own, down_other, flipped=True, scale=slope)
    up_given = swap_core(line.run(grads, normed, back, right_half=1))
    between(1)
    send_down(line.run(grads, hidden, grad, left_half=0, more=down_given))
    normed_grad = line.run(both, back, up_own, up_other, flipped=True)
    send_up(line.run(grads, normed, back, right_half=0, more=up_given))
    stream_grad, gain_grad, shift_grad = norm_backward(normed_grad, unit, inverse, gain)
    return (grad + stream_grad, gain_grad, shift_grad)


def local_moments(grad, rows_old, weight):
    squared = grad * grad + TINY
    rows_new = DECAY * rows_old + (1.0 - DECAY) * jnp.mean(squared, axis=1)
    scaled = jnp.sum(grad * grad / rows_new[:, None], axis=0)
    pair = jnp.stack([jnp.sum(rows_new), jnp.sum(weight * weight)])
    return (rows_new, [jnp.sum(squared, axis=0), scaled, pair])


def finish(grad, weight, rows_new, cols_old, totals, total_rows):
    column_total, scaled_total, pair = totals
    cols_new = DECAY * cols_old + (1.0 - DECAY) * (column_total / total_rows)
    rows_mean = pair[0] / total_rows
    second = rows_new[:, None] * cols_new[None, :] / rows_mean
    update = grad * lax.rsqrt(second)
    count = total_rows * grad.shape[1]
    ratio = jnp.sqrt(rows_mean * jnp.sum(scaled_total / cols_new) / count) / CLIP
    scale = jnp.maximum(jnp.sqrt(pair[1] / count), FLOOR)
    return (cols_new, weight - RHO * scale * (update / jnp.maximum(ratio, 1.0)))


def on_device(
    frames,
    cotangent,
    lengths,
    attn_in,
    attn_out,
    ffn_up,
    ffn_down,
    norm_params,
    skip_proj,
    in_rows,
    in_cols,
    out_rows,
    out_cols,
    up_rows,
    up_cols,
    down_rows,
    down_cols,
    skip_rows,
    skip_cols,
    norm_moment,
):
    section = lax.axis_index("section")
    me = lax.axis_index("dp")
    data_size = lax.axis_size("dp")
    first = section == 0
    frame_count, model_width = frames.shape[2], frames.shape[3]
    width = model_width // 2
    share = attn_in.shape[1]
    hidden_block = ffn_down.shape[1] // 2
    lanes = 2 * model_width // HEADS
    source = lax.dynamic_index_in_dim(frames, section, 0, keepdims=False)[0]
    length = lax.dynamic_index_in_dim(lengths, section, 0, keepdims=False)[0]
    valid_rows = (jnp.arange(frame_count) < length).astype(jnp.float32)[:, None]
    outer = lax.dynamic_index_in_dim(cotangent, section, 0, keepdims=False)[0] * valid_rows

    def attn_half(s):
        split = attn_in[0].reshape(share, 3, 2, -1, lanes)
        inner = lax.dynamic_index_in_dim(split, s, 2, keepdims=False).swapaxes(1, 2)
        outward = lax.dynamic_slice_in_dim(attn_out[0], s * width, width, 1)
        return jnp.concatenate([inner.reshape(share, 3 * width), outward], 1)

    def up_half(shard, s):
        split = shard[0].reshape(share, data_size, 2, hidden_block)
        return lax.dynamic_index_in_dim(split, s, 2, keepdims=False).reshape(share, -1)

    def down_half(shard, s):
        return lax.dynamic_slice_in_dim(shard[0], s * hidden_block, hidden_block, 0)

    def by_owner(half):
        kept = half(section)
        given = swap_core(half(1 - section))
        return (jnp.where(first, kept, given), jnp.where(first, given, kept))

    norm_shard = jnp.pad(norm_params[0].T, ((0, 0), (0, PAD - norm_params.shape[1])))
    attn_zero, attn_one = by_owner(attn_half)
    attn_zero = jnp.concatenate([attn_zero, norm_shard], 1)
    (ffn_up_held, ffn_down_held), _ = lax.optimization_barrier(((ffn_up, ffn_down), attn_zero))
    up_zero, up_one = by_owner(partial(up_half, ffn_up_held))
    down_zero, down_one = by_owner(partial(down_half, ffn_down_held))
    gather = Gather([attn_zero, down_one, skip_proj, attn_one])

    def gather_beside(shard, *needs):
        whole = lax.all_gather(shard, "dp", axis=0, tiled=True)
        return (whole, swap_core(hold(whole, *needs)))

    line = Line()
    for _ in range(5):
        gather.turn()
    attn_zero_full = gather.wholes[0]
    norms = [full[:, 4 * width : 4 * width + 4].T for full in attn_zero_full]
    norm_zero = jnp.where(first, norms[0], norms[1])
    norm_one = jnp.where(first, norms[1], norms[0])
    after_attn, saved_a0 = attention_forward(
        source, norm_zero[0], norm_zero[1], attn_zero_full, length, line
    )
    gather.turn(after_attn)
    ffn_one_full = gather_beside(up_one) + gather.wholes[1]
    finish_twelve, saved_f1 = feed_forward(
        after_attn, norm_one[2], norm_one[3], ffn_one_full, line
    )
    twelve = finish_twelve()
    gather.turn(twelve)
    skip_full, attn_one_full = gather.wholes[2:]
    joined_own = jnp.where(first, twelve, source)
    joined_other = jnp.where(first, source, twelve)
    joined = line.run(both, (joined_own, joined_other), *skip_full)
    middle, saved_a1 = attention_forward(
        joined, norm_one[0], norm_one[1], attn_one_full, length, line
    )
    ffn_zero_full = gather_beside(up_zero) + gather_beside(down_zero, joined)
    finish_thirteen, saved_f0 = feed_forward(
        middle, norm_zero[2], norm_zero[3], ffn_zero_full, line
    )

    sums = Sums()
    late = []

    def send(summed):
        line.need(*sums.turn(summed))

    def under_way():
        return sums.sent.get("xy", ()) + ((sums.sent["far"],) if "far" in sums.sent else ())

    def between(step):
        return None

    grad, g02, g03 = feed_backward(
        outer, saved_f0, ffn_zero_full, line, between, send, send
    )
    thirteen = finish_thirteen()
    grad, g10, g11 = attention_backward(grad, saved_a1, attn_one_full, length, line, send, under_way)
    skip_given = swap_core(line.run(grads, joined_other, grad))
    back = line.run(wide, grad, *skip_full, flipped=True, by_section=True)
    joined_grad = grad
    grad, frames_grad = back[:, :model_width], back[:, model_width:]

    def between(step):
        if step == 0:
            late.append(line.run(grads, joined_own, joined_grad, more=skip_given))
            line.need(*under_way())
        else:
            send(late[0])

    grad, g12, g13 = feed_backward(grad, saved_f1, ffn_one_full, line, between, send, send)
    after_attn_grad = grad
    grad, g00, g01 = attention_backward(grad, saved_a0, attn_zero_full, length, line, send, under_way)
    frames_grad = frames_grad + grad
    norm_grads = total_dp(jnp.stack([g00, g01, g02, g03, g10, g11, g12, g13]))
    norm_grads = (norm_grads + swap_core(norm_grads)).reshape(2, 4, model_width)
    norm_share = lax.dynamic_slice(norm_grads, (section, 0, me * share), (1, 4, share))[0]
    for _ in range(3):
        sums.turn()
    sums.close()
    down_zero_s, up_zero_s, attn_one_s, skip_grad, down_one_s, up_one_s, attn_zero_s = sums.totals

    def to_owner(zero, one):
        kept = jnp.where(first, zero, one)
        given = swap_core(jnp.where(first, one, zero))
        return (jnp.where(first, kept, given), jnp.where(first, given, kept))

    def in_columns(part):
        split = part[:, : 3 * width].reshape(share, -1, 3, lanes).swapaxes(1, 2)
        return split.reshape(share, 3, width)

    attn_pair = to_owner(attn_zero_s, attn_one_s)
    up_pair = to_owner(up_zero_s, up_one_s)
    shares = [
        jnp.stack([in_columns(part) for part in attn_pair], 2).reshape(share, -1),
        jnp.concatenate([part[:, 3 * width :] for part in attn_pair], 1),
        jnp.stack([part.reshape(share, data_size, -1) for part in up_pair], 2).reshape(share, -1),
        jnp.concatenate(to_owner(down_zero_s, down_one_s), 0),
    ]

    current = [attn_in[0], attn_out[0], ffn_up[0], ffn_down[0]]
    rows_old = [in_rows[0], out_rows[0], up_rows[0], down_rows[0]]
    cols_old = [in_cols[0], out_cols[0], up_cols[0], down_cols[0]]
    moments = [local_moments(g, r, w) for g, r, w in zip(shares, rows_old, current)]
    skip_rows_new, skip_local = local_moments(skip_grad, skip_rows, skip_proj)
    norm_moment_new = DECAY * norm_moment[0] + (1.0 - DECAY) * (norm_share * norm_share + TINY)
    norm_raw = norm_share * lax.rsqrt(norm_moment_new)
    norm_sums = [
        jnp.sum(norm_raw * norm_raw, axis=-1),
        jnp.sum(norm_params[0] * norm_params[0], axis=-1),
    ]
    vectors = skip_local + [v for _, local in moments for v in local] + norm_sums
    sizes = [v.shape[0] for v in vectors]
    packed = jnp.concatenate(vectors)
    packed = total_dp(jnp.pad(packed, (0, -packed.shape[0] % PAD)))
    skip_size = sum(sizes[:3])
    skip_totals = packed[:skip_size] + swap_core(packed[:skip_size])
    offsets = [sum(sizes[:k]) for k in range(len(sizes))]
    totals = [packed[at : at + size] for at, size in zip(offsets, sizes)]
    updated = [
        finish(
            shares[k],
            current[k],
            moments[k][0],
            cols_old[k],
            totals[3 + 3 * k : 6 + 3 * k],
            shares[k].shape[0] * data_size,
        )
        for k in range(4)
    ]
    skip_cols_new, skip_new = finish(
        skip_grad,
        skip_proj,
        skip_rows_new,
        skip_cols,
        [skip_totals[at : at + size] for at, size in zip(offsets[:3], sizes[:3])],
        skip_grad.shape[0] * data_size * 2,
    )
    norm_ratio = jnp.sqrt(totals[15] / model_width) / CLIP
    norm_scale = jnp.maximum(jnp.sqrt(totals[16] / model_width), FLOOR)
    norms_new = norm_params[0] - RHO * norm_scale[:, None] * (
        norm_raw / jnp.maximum(norm_ratio, 1.0)[:, None]
    )

    def both_micro(zero, one):
        kept = jnp.where(first, zero, one)
        given = swap_core(jnp.where(first, one, zero))
        pair = jnp.where(first, jnp.stack([kept, given]), jnp.stack([given, kept]))
        return pair[None, :, None]

    layer_outputs = both_micro(thirteen, twelve)
    input_grads = both_micro(frames_grad, after_attn_grad)
    return (
        layer_outputs,
        input_grads,
        shares[0][None],
        moments[0][0][None],
        updated[0][0][None],
        updated[0][1][None],
        shares[1][None],
        moments[1][0][None],
        updated[1][0][None],
        updated[1][1][None],
        shares[2][None],
        moments[2][0][None],
        updated[2][0][None],
        updated[2][1][None],
        shares[3][None],
        moments[3][0][None],
        updated[3][0][None],
        updated[3][1][None],
        skip_grad,
        skip_rows_new,
        skip_cols_new,
        skip_new,
        norm_share[None],
        norm_moment_new[None],
        norms_new[None],
    )


def solution(mesh):
    return jax.shard_map(
        on_device,
        mesh=mesh,
        in_specs=(
            P(None, "dp", None, None),
            P(None, "dp", None, None),
            P(None, "dp"),
            P("section", "dp", None),
            P("section", "dp", None),
            P("section", "dp", None),
            P("section", "dp", None),
            P("section", None, "dp"),
            P(("section", "dp"), None),
            P("section", "dp"),
            P("section", None),
            P("section", "dp"),
            P("section", None),
            P("section", "dp"),
            P("section", None),
            P("section", "dp"),
            P("section", None),
            P(("section", "dp")),
            P(),
            P("section", None, "dp"),
        ),
        out_specs=(
            P("section", None, "dp", None, None),
            P("section", None, "dp", None, None),
            P("section", "dp", None),
            P("section", "dp"),
            P("section", None),
            P("section", "dp", None),
            P("section", "dp", None),
            P("section", "dp"),
            P("section", None),
            P("section", "dp", None),
            P("section", "dp", None),
            P("section", "dp"),
            P("section", None),
            P("section", "dp", None),
            P("section", "dp", None),
            P("section", "dp"),
            P("section", None),
            P("section", "dp", None),
            P(("section", "dp"), None),
            P(("section", "dp")),
            P(),
            P(("section", "dp"), None),
            P("section", None, "dp"),
            P("section", None, "dp"),
            P("section", None, "dp"),
        ),
        check_vma=False,
    )
```
